32 devices in a mesh: tm: 8 (over z, core), head: 4 (over y, x).
Axes of the slice: x: 2, y: 2, z: 4, core: 2. Of those that a mesh axis runs over, the one named last changes fastest.
Arguments:
- queries: bfloat16 [8192, 2048], P(('tm', 'head')), may hold values from -200 to 200
- key_rows: bfloat16 [8192, 2048], P(('tm', 'head')), may hold values from -6 to 6
- value_rows: bfloat16 [8192, 2048], P(('tm', 'head')), may hold values from -6 to 6
- grad_out: bfloat16 [8192, 2048], P(('tm', 'head')), may hold values from -6 to 6
- tile_lists: int32 [64, 17], replicated, may hold values from -1 to 63, as said below
Outputs:
- attended: bfloat16 [8192, 2048], P(('tm', 'head'))
- grad_queries: bfloat16 [8192, 2048], P(('tm', 'head'))
- grad_keys: bfloat16 [8192, 2048], P(('tm', 'head'))
- grad_values: bfloat16 [8192, 2048], P(('tm', 'head'))
The draws below stay inside these ranges and needn't reach their ends.
Inputs may be any that keep to these rules, and one draw needn't show every extreme that they name: Row i of tile_lists holds i + o for each of 17 offsets o, in the same order in every row; the offsets are distinct, 0, 1, -1, 32 and -(32) among them, and o is one of them exactly when -o is; the entry is -1 where i + o lies outside 0 to 63.
All inputs are finite; a program needn't handle non-finite values.
Results may differ from the reference program's by a relative error of at most 0.03.
Values may be sent and summed in bfloat16 or wider, within the bound.
A program may use at most 384 MiB of HBM per device.

```python
import jax
import jax.numpy as jnp
from jax import lax

HEAD_DIM = 128
HEADS = 16
BLOCK = 128
HALF = 8
KPR = 17
TOKENS = 8192
NB = 64


def shared_keys(key):
    return jnp.clip(jax.random.normal(key, (TOKENS, HEADS * HEAD_DIM), jnp.float32), -6.0, 6.0)


def draw_key_rows(key, part):
    base = shared_keys(key)
    return base.astype(jnp.bfloat16)


def draw_queries(key, part):
    key = jax.random.fold_in(key, 1)
    fresh = jnp.clip(jax.random.normal(key, (TOKENS, HEADS * HEAD_DIM), jnp.float32), -6.0, 6.0)
    return fresh.astype(jnp.bfloat16)


def draw_tile_lists(key, part):
    key = jax.random.fold_in(key, 3)
    middle = NB // 2
    distances = jnp.arange(2, NB, dtype=jnp.int32)
    rolled = jax.random.randint(key, (NB - 2,), 0, 1048576, dtype=jnp.int32)
    ranking = rolled // distances * NB + distances
    ranking = jnp.where(distances == middle, -1, ranking)
    picked = lax.top_k(ranking, HALF - 2)[1]
    chosen = jnp.concatenate([distances[picked], jnp.full((1,), middle, jnp.int32)])
    positive = jnp.concatenate([jnp.ones((1,), jnp.int32), jnp.sort(chosen)])
    offsets = jnp.concatenate([-positive[::-1], jnp.zeros((1,), jnp.int32), positive])
    targets = jnp.arange(NB, dtype=jnp.int32)[:, None] + offsets[None, :]
    inside = (targets >= 0) & (targets < NB)
    return jnp.where(inside, targets, -1).astype(jnp.int32)


def block_levels(rng, extent, pieces, least, high):
    loudness = 1.0
    for position, parts in pieces:
        draws = jax.random.uniform(jax.random.fold_in(jax.random.fold_in(rng, 6), position), (parts,), jnp.float32, least / len(pieces), high / len(pieces))
        loudness = loudness * jnp.repeat(jnp.exp(draws), extent[position] // parts).reshape((-1,) + (1,) * (len(extent) - 1 - position))
    return loudness


def normal_values(rng, shape, width, bound, cuts=(), held_as=jnp.bfloat16):
    values = jax.random.normal(rng, shape, jnp.float32) * width
    if len(cuts) > 0:
        values = block_levels(rng, shape, cuts, -0.22, 0.18) * values
    return jnp.clip(values, min=-bound, max=bound).astype(held_as)


def setup_inputs(seed: int = 0) -> dict:
    key_list = jax.random.split(jax.random.key(seed), 6)
    return {
        "queries": draw_queries(jax.random.fold_in(key_list[5], 71), 0),
        "key_rows": draw_key_rows(jax.random.fold_in(key_list[5], 71), 0),
        "value_rows": normal_values(key_list[2], (TOKENS, HEADS * HEAD_DIM), 1.0, 6.0, ((0, 32),)),
        "grad_out": normal_values(key_list[3], (TOKENS, HEADS * HEAD_DIM), 1.0, 6.0, ((0, 32),)),
        "tile_lists": draw_tile_lists(jax.random.fold_in(key_list[5], 71), 0),
    }


def by_head(tensor):
    return tensor.reshape(NB, BLOCK, HEADS, HEAD_DIM).transpose(2, 0, 1, 3)


def join_heads(tensor):
    return tensor.transpose(1, 2, 0, 3).reshape(TOKENS, HEADS * HEAD_DIM)


def reference(queries, key_rows, value_rows, grad_out, tile_lists):
    scaling = HEAD_DIM ** -0.5
    live_slot = tile_lists >= 0
    slot_tile = jnp.maximum(tile_lists, 0).astype(jnp.int32)

    def one_head(operands):
        query_head, key_head, value_head, grad_head = operands

        def one_tile(carry, inputs):
            key_acc, value_acc = carry
            query_tile, grad_tile, chosen, live = inputs
            keys_sel = key_head[chosen].reshape(KPR * BLOCK, HEAD_DIM)
            values_sel = value_head[chosen].reshape(KPR * BLOCK, HEAD_DIM)
            live_cols = jnp.repeat(live, BLOCK)
            scores = jnp.dot(query_tile, keys_sel.T, preferred_element_type=jnp.float32) * scaling
            scores = jnp.where(live_cols[None, :], scores, -jnp.inf)
            row_top = jnp.max(scores, axis=-1, keepdims=True)
            row_total = jnp.sum(jnp.exp(scores - row_top), axis=-1, keepdims=True)
            log_total = row_top + jnp.log(row_total)
            prob_rows = jnp.exp(scores - log_total)
            weights = prob_rows.astype(jnp.bfloat16)
            attended = jnp.dot(weights, values_sel, preferred_element_type=jnp.float32).astype(jnp.bfloat16)
            row_delta = jnp.sum(attended.astype(jnp.float32) * grad_tile.astype(jnp.float32), axis=-1, keepdims=True)
            dprob_rows = jnp.dot(grad_tile, values_sel.T, preferred_element_type=jnp.float32)
            dscore = (prob_rows * (dprob_rows - row_delta)).astype(jnp.bfloat16)
            grad_query = (jnp.dot(dscore, keys_sel, preferred_element_type=jnp.float32) * scaling).astype(jnp.bfloat16)
            key_part = jnp.dot(dscore.T, query_tile, preferred_element_type=jnp.float32)
            value_part = jnp.dot(weights.T, grad_tile, preferred_element_type=jnp.float32)
            key_acc = key_acc.at[chosen].add(key_part.reshape(KPR, BLOCK, HEAD_DIM))
            value_acc = value_acc.at[chosen].add(value_part.reshape(KPR, BLOCK, HEAD_DIM))
            return (key_acc, value_acc), (attended, grad_query)

        zeros = jnp.zeros((NB, BLOCK, HEAD_DIM), jnp.float32)
        sums, outputs = lax.scan(one_tile, (zeros, zeros), (query_head, grad_head, slot_tile, live_slot))
        grad_key = (sums[0] * scaling).astype(jnp.bfloat16)
        grad_value = sums[1].astype(jnp.bfloat16)
        return outputs[0], outputs[1], grad_key, grad_value

    results = lax.map(one_head, (by_head(queries), by_head(key_rows), by_head(value_rows), by_head(grad_out)))
    return (join_heads(results[0]), join_heads(results[1]), join_heads(results[2]), join_heads(results[3]))
```

```python
import functools
import math

import jax
import jax.numpy as jnp
from jax import lax
from jax.experimental import pallas as pl
from jax.experimental.pallas import tpu as pltpu
from jax.sharding import PartitionSpec as P

HEAD_DIM = 128
HEADS = 16
BLOCK = 128
CHUNK = 4
PAIR = 2
DEPTHS = 5
MESH = pl.DeviceIdType.MESH
MIB = 1024 * 1024


def slab_stack(doubled, start_tile, offsets, group, tile_total, slot_count):
    pieces = []
    for slot in range(slot_count):
        where_at = jnp.mod(start_tile + offsets[slot], tile_total)
        pieces.append(lax.dynamic_slice_in_dim(doubled, where_at, group, 0))
    return jnp.stack(pieces, 0)


def add_slabs(accum, parts, start_tile, offsets, group, tile_total, slot_count):
    for slot in range(slot_count):
        where_at = jnp.mod(start_tile + offsets[slot], tile_total)
        current = lax.dynamic_slice_in_dim(accum, where_at, group, 0)
        accum = lax.dynamic_update_slice_in_dim(accum, current + parts[slot], where_at, 0)
    return accum


def on_device(queries, key_rows, value_rows, grad_out, tile_lists):
    heads_here = HEADS // lax.axis_size("head")
    arrived = (
        lax.all_to_all(queries, "head", split_axis=1, concat_axis=0, tiled=True),
        lax.all_to_all(key_rows, "head", split_axis=1, concat_axis=0, tiled=True),
        lax.all_to_all(value_rows, "head", split_axis=1, concat_axis=0, tiled=True),
        lax.all_to_all(grad_out, "head", split_axis=1, concat_axis=0, tiled=True),
    )
    tokens_here = arrived[0].shape[0]
    query_loc = arrived[0].reshape(tokens_here, heads_here, HEAD_DIM)
    key_loc = arrived[1].reshape(tokens_here, heads_here, HEAD_DIM)
    value_loc = arrived[2].reshape(tokens_here, heads_here, HEAD_DIM)
    grad_loc = arrived[3].reshape(tokens_here, heads_here, HEAD_DIM)
    scaling = HEAD_DIM ** (-0.5)
    local_tiles = tokens_here // BLOCK
    tile_total = tile_lists.shape[0]
    slot_count = tile_lists.shape[1]
    group = math.gcd(local_tiles, max(1, 512 // BLOCK))
    group_count = local_tiles // group
    first_tile = lax.axis_index("tm") * local_tiles
    row_index = jnp.arange(tile_total, dtype=jnp.int32)[:, None]
    offsets = jnp.max(jnp.where(tile_lists >= 0, tile_lists - row_index, -2 * tile_total), axis=0)
    own_lists = lax.dynamic_slice_in_dim(tile_lists, first_tile, local_tiles, 0)
    live_slot = own_lists >= 0
    whole_keys, whole_values = (
        lax.all_gather(key_loc, "tm", axis=0, tiled=True),
        lax.all_gather(value_loc, "tm", axis=0, tiled=True),
    )
    key_tiles = whole_keys.reshape(tile_total, BLOCK, heads_here, HEAD_DIM)
    value_tiles = whole_values.reshape(tile_total, BLOCK, heads_here, HEAD_DIM)
    doubled_keys = jnp.concatenate([key_tiles, key_tiles], 0)
    doubled_values = jnp.concatenate([value_tiles, value_tiles], 0)
    query_tiles = query_loc.reshape(local_tiles, BLOCK, heads_here, HEAD_DIM)
    grad_tiles = grad_loc.reshape(local_tiles, BLOCK, heads_here, HEAD_DIM)

    def forward_group(group_idx):
        offset_loc = group_idx * group
        start_tile = first_tile + offset_loc
        query_tile = lax.dynamic_slice_in_dim(query_tiles, offset_loc, group, 0)
        grad_tile = lax.dynamic_slice_in_dim(grad_tiles, offset_loc, group, 0)
        live = lax.dynamic_slice_in_dim(live_slot, offset_loc, group, 0)
        keys_sel = slab_stack(doubled_keys, start_tile, offsets, group, tile_total, slot_count)
        values_sel = slab_stack(doubled_values, start_tile, offsets, group, tile_total, slot_count)
        live_mask = live[:, None, None, :, None]
        scores = (
            jnp.einsum(
                "tqhd,stkhd->thqsk", query_tile, keys_sel, preferred_element_type=jnp.float32
            )
            * scaling
        )
        scores = jnp.where(live_mask, scores, -jnp.inf)
        row_top = jnp.max(scores, axis=(3, 4), keepdims=True)
        row_total = jnp.sum(jnp.exp(scores - row_top), axis=(3, 4), keepdims=True)
        log_total = row_top + jnp.log(row_total)
        prob_rows = jnp.exp(scores - log_total)
        weights = prob_rows.astype(jnp.bfloat16)
        attended = jnp.einsum(
            "thqsk,stkhd->tqhd", weights, values_sel, preferred_element_type=jnp.float32
        ).astype(jnp.bfloat16)
        row_delta = jnp.sum(attended.astype(jnp.float32) * grad_tile.astype(jnp.float32), axis=-1)
        dprob_rows = jnp.einsum(
            "tqhd,stkhd->thqsk", grad_tile, values_sel, preferred_element_type=jnp.float32
        )
        dscore = (
            prob_rows * (dprob_rows - row_delta.transpose(0, 2, 1)[:, :, :, None, None])
        ).astype(jnp.bfloat16)
        grad_query = (
            jnp.einsum("thqsk,stkhd->tqhd", dscore, keys_sel, preferred_element_type=jnp.float32)
            * scaling
        ).astype(jnp.bfloat16)
        return (
            start_tile,
            query_tile,
            grad_tile,
            attended,
            grad_query,
            log_total[:, :, :, 0, 0],
            row_delta,
            weights,
            dscore,
        )

    group_ids = jnp.arange(group_count, dtype=jnp.int32)

    def group_with_sums(carry, group_idx):
        key_acc, value_acc = carry
        (
            start_tile,
            query_tile,
            grad_tile,
            attended,
            grad_query,
            log_total,
            row_delta,
            weights,
            dscore,
        ) = forward_group(group_idx)
        key_part = jnp.einsum(
            "thqsk,tqhd->stkhd", dscore, query_tile, preferred_element_type=jnp.float32
        )
        value_part = jnp.einsum(
            "thqsk,tqhd->stkhd", weights, grad_tile, preferred_element_type=jnp.float32
        )
        key_acc = add_slabs(key_acc, key_part, start_tile, offsets, group, tile_total, slot_count)
        value_acc = add_slabs(
            value_acc, value_part, start_tile, offsets, group, tile_total, slot_count
        )
        return ((key_acc, value_acc), (attended, grad_query))

    zeros = jnp.zeros((2 * tile_total, BLOCK, heads_here, HEAD_DIM), jnp.float32)
    sums, outputs = lax.scan(group_with_sums, (zeros, zeros), group_ids)
    key_fold = sums[0][:tile_total] + sums[0][tile_total:]
    value_fold = sums[1][:tile_total] + sums[1][tile_total:]
    whole_rows = tile_total * BLOCK
    key_sum, value_sum = (
        lax.psum_scatter(
            key_fold.reshape(whole_rows, heads_here, HEAD_DIM).astype(jnp.bfloat16),
            "tm",
            scatter_dimension=0,
            tiled=True,
        ).astype(jnp.float32),
        lax.psum_scatter(
            value_fold.reshape(whole_rows, heads_here, HEAD_DIM).astype(jnp.bfloat16),
            "tm",
            scatter_dimension=0,
            tiled=True,
        ).astype(jnp.float32),
    )
    attended = outputs[0].reshape(tokens_here, heads_here, HEAD_DIM)
    grad_query = outputs[1].reshape(tokens_here, heads_here, HEAD_DIM)
    grad_key = (key_sum * scaling).astype(jnp.bfloat16)
    grad_value = value_sum.astype(jnp.bfloat16)
    width = heads_here * HEAD_DIM
    results = (
        lax.all_to_all(
            attended.reshape(tokens_here, width), "head", split_axis=0, concat_axis=1, tiled=True
        ),
        lax.all_to_all(
            grad_query.reshape(tokens_here, width), "head", split_axis=0, concat_axis=1, tiled=True
        ),
        lax.all_to_all(
            grad_key.reshape(tokens_here, width), "head", split_axis=0, concat_axis=1, tiled=True
        ),
        lax.all_to_all(
            grad_value.reshape(tokens_here, width), "head", split_axis=0, concat_axis=1, tiled=True
        ),
    )
    return (results[0], results[1], results[2], results[3])


def place(pos, core, z_size):
    return (2 * lax.rem(pos, z_size) + core, lax.div(pos, z_size))


def slot_of(pos, z_size, hd_size):
    return lax.rem(pos, z_size) * hd_size + lax.div(pos, z_size)


def columns_of(pos):
    return pl.ds(pl.multiple_of(pos * HEAD_DIM, HEAD_DIM), HEAD_DIM)


def block_rows(index, rows):
    return pl.ds(pl.multiple_of(index * rows, rows), rows)


def greet(count, pos, core, z_size, tm, hd):
    barrier = pltpu.get_barrier_semaphore()

    def signal(step, carry):
        other = lax.rem(pos + step, count)
        pl.semaphore_signal(
            barrier, inc=1, device_id=place(other, core, z_size), device_id_type=MESH
        )
        return carry

    lax.fori_loop(1, count, signal, 0)
    pl.semaphore_signal(
        barrier, inc=1, device_id=(tm + 1 - 2 * core, hd), device_id_type=MESH
    )
    pl.semaphore_wait(barrier, count)


def scatter_kernel(
    tm_size, hd_size, q_ref, k_ref, v_ref, g_ref, qg_ref, kv_ref,
    send, recv, pair_send, pair_recv, own_sem,
):
    z_size = tm_size // 2
    count = z_size * hd_size
    rows = q_ref.shape[0]
    tm, hd = lax.axis_index("tm"), lax.axis_index("head")
    core = lax.rem(tm, 2)
    pos = hd * z_size + lax.div(tm, 2)
    sibling = (tm + 1 - 2 * core, hd)
    greet(count, pos, core, z_size, tm, hd)

    left, right = pl.ds(0, HEAD_DIM), pl.ds(HEAD_DIM, HEAD_DIM)
    sources = (k_ref, v_ref, q_ref, g_ref)

    def global_block(where):
        tm_of, hd_of = place(where, core, z_size)
        return tm_of * hd_size + hd_of

    def landing(tensor, where):
        half = left if tensor % 2 == 0 else right
        if tensor < 2:
            return kv_ref.at[block_rows(global_block(where), rows), half]
        return qg_ref.at[block_rows(slot_of(where, z_size, hd_size), rows), half]

    def outgoing(tensor, target):
        return pltpu.make_async_remote_copy(
            src_ref=sources[tensor].at[:, columns_of(target)],
            dst_ref=landing(tensor, pos),
            send_sem=send.at[tensor, target],
            recv_sem=recv.at[tensor, pos],
            device_id=place(target, core, z_size),
            device_id_type=MESH,
        )

    def incoming(tensor, origin):
        return pltpu.make_async_remote_copy(
            src_ref=sources[tensor].at[:, columns_of(pos)],
            dst_ref=landing(tensor, origin),
            send_sem=send.at[tensor, origin],
            recv_sem=recv.at[tensor, origin],
            device_id=place(origin, core, z_size),
            device_id_type=MESH,
        )

    def to_sibling(where):
        block = kv_ref.at[block_rows(global_block(where), rows), :]
        return pltpu.make_async_remote_copy(
            src_ref=block, dst_ref=block,
            send_sem=pair_send.at[where], recv_sem=pair_recv.at[where],
            device_id=sibling, device_id_type=MESH,
        )

    def from_sibling(where):
        tm_of, hd_of = place(where, 1 - core, z_size)
        block = kv_ref.at[block_rows(tm_of * hd_size + hd_of, rows), :]
        return pltpu.make_async_remote_copy(
            src_ref=block, dst_ref=block,
            send_sem=pair_send.at[where], recv_sem=pair_recv.at[where],
            device_id=sibling, device_id_type=MESH,
        )

    def send_pair(first):
        def step_body(step, carry):
            target = lax.rem(pos + step, count)
            outgoing(first, target).start()
            outgoing(first + 1, target).start()
            return carry

        lax.fori_loop(1, count, step_body, 0)

    own = [
        pltpu.make_async_copy(
            sources[tensor].at[:, columns_of(pos)],
            landing(tensor, pos),
            own_sem.at[tensor],
        )
        for tensor in range(4)
    ]
    for copy in own:
        copy.start()
    send_pair(0)
    send_pair(2)
    own[0].wait()
    own[1].wait()
    to_sibling(pos).start()

    def forward(step, carry):
        origin = lax.rem(pos + count - step, count)
        incoming(0, origin).wait_recv()
        incoming(1, origin).wait_recv()
        to_sibling(origin).start()
        return carry

    lax.fori_loop(1, count, forward, 0)
    own[2].wait()
    own[3].wait()

    def finish(step, carry):
        other = lax.rem(pos + count - step, count)
        incoming(2, other).wait_recv()
        incoming(3, other).wait_recv()
        for tensor in range(4):
            outgoing(tensor, other).wait_send()
        return carry

    lax.fori_loop(1, count, finish, 0)

    def finish_pair(where, carry):
        from_sibling(where).wait_recv()
        to_sibling(where).wait_send()
        return carry

    lax.fori_loop(0, count, finish_pair, 0)


def return_kernel(
    tm_size, hd_size, o_ref, dq_ref, mine_ref, theirs_ref,
    o_out, dq_out, dk_out, dv_out,
    landed, total, send, recv, pair_send, pair_recv, own_sem,
):
    z_size = tm_size // 2
    count = z_size * hd_size
    rows = o_out.shape[0]
    tm, hd = lax.axis_index("tm"), lax.axis_index("head")
    core = lax.rem(tm, 2)
    pos = hd * z_size + lax.div(tm, 2)
    sibling = (tm + 1 - 2 * core, hd)
    greet(count, pos, core, z_size, tm, hd)

    left, right = pl.ds(0, HEAD_DIM), pl.ds(HEAD_DIM, HEAD_DIM)
    outs = (o_out, dq_out, dv_out, dk_out)

    def source(tensor, where):
        if tensor < 2:
            return (o_ref, dq_ref)[tensor].at[block_rows(slot_of(where, z_size, hd_size), rows), :]
        return total.at[block_rows(slot_of(where, z_size, hd_size), rows), left if tensor == 2 else right]

    def outgoing(tensor, target):
        return pltpu.make_async_remote_copy(
            src_ref=source(tensor, target),
            dst_ref=outs[tensor].at[:, columns_of(pos)],
            send_sem=send.at[tensor, target],
            recv_sem=recv.at[tensor, pos],
            device_id=place(target, core, z_size),
            device_id_type=MESH,
        )

    def incoming(tensor, origin):
        return pltpu.make_async_remote_copy(
            src_ref=source(tensor, origin),
            dst_ref=outs[tensor].at[:, columns_of(origin)],
            send_sem=send.at[tensor, origin],
            recv_sem=recv.at[tensor, origin],
            device_id=place(origin, core, z_size),
            device_id_type=MESH,
        )

    def pair(where):
        return pltpu.make_async_remote_copy(
            src_ref=theirs_ref.at[block_rows(slot_of(where, z_size, hd_size), rows), :],
            dst_ref=landed.at[block_rows(slot_of(where, z_size, hd_size), rows), :],
            send_sem=pair_send.at[where], recv_sem=pair_recv.at[where],
            device_id=sibling, device_id_type=MESH,
        )

    def own(tensor):
        return pltpu.make_async_copy(
            source(tensor, pos),
            outs[tensor].at[:, columns_of(pos)],
            own_sem.at[tensor],
        )

    def start_pair(step, carry):
        pair(lax.rem(pos + step, count)).start()
        return carry

    lax.fori_loop(1, count + 1, start_pair, 0)

    def start_first(step, carry):
        target = lax.rem(pos + step, count)
        outgoing(0, target).start()
        outgoing(1, target).start()
        return carry

    lax.fori_loop(1, count, start_first, 0)
    own(0).start()
    own(1).start()

    def add(where):
        pair(where).wait_recv()
        here = block_rows(slot_of(where, z_size, hd_size), rows)
        total[here, :] = (mine_ref[here, :] + landed[here, :].astype(jnp.float32)).astype(
            jnp.bfloat16
        )

    def start_second(step, carry):
        target = lax.rem(pos + step, count)
        add(target)
        outgoing(2, target).start()
        outgoing(3, target).start()
        return carry

    lax.fori_loop(1, count, start_second, 0)
    add(pos)
    own(2).start()
    own(3).start()
    for tensor in range(4):
        own(tensor).wait()

    def finish(step, carry):
        other = lax.rem(pos + count - step, count)
        for tensor in range(4):
            incoming(tensor, other).wait_recv()
            outgoing(tensor, other).wait_send()
        return carry

    lax.fori_loop(1, count, finish, 0)

    def finish_pair(where, carry):
        pair(where).wait_send()
        return carry

    lax.fori_loop(0, count, finish_pair, 0)


def attend_kernel(
    tiles_per_shard, slots, lists_ref, counts_ref, core_ref, qg_ref, kv_ref,
    o_ref, dq_ref, mine_ref, theirs_ref,
    kv_t, scores, sums, read_w, sum_w,
):
    scaling = HEAD_DIM ** (-0.5)
    step = pl.program_id(0)
    tile_total = kv_ref.shape[0] // BLOCK

    @pl.when(step == 0)
    def _():
        def turn(tile, carry):
            kv_t[:, block_rows(tile, BLOCK)] = kv_ref[block_rows(tile, BLOCK), :].T
            sums[block_rows(tile, BLOCK), :] = jnp.zeros((BLOCK, 2 * HEAD_DIM), jnp.float32)
            return carry

        lax.fori_loop(0, tile_total, turn, 0)
        read_w[...] = jnp.zeros_like(read_w)
        sum_w[...] = jnp.zeros_like(sum_w)

    live = [counts_ref[step * PAIR + sub] for sub in range(PAIR)]
    most = live[0]
    for sub in range(1, PAIR):
        most = jnp.maximum(most, live[sub])
    rate = scaling * math.log2(math.e)

    def read(sub, depth):
        rows = slice(sub * BLOCK, (sub + 1) * BLOCK)
        query, grad = qg_ref[rows, :HEAD_DIM], qg_ref[rows, HEAD_DIM:]
        read_w[sub, :BLOCK, :HEAD_DIM] = query
        read_w[sub, BLOCK:, HEAD_DIM:] = grad
        sum_w[sub, :BLOCK, :HEAD_DIM] = grad
        sum_w[sub, BLOCK:, HEAD_DIM:] = query
        base = (step * PAIR + sub) * slots
        tiles = [lists_ref[base + j] for j in range(depth)]
        top = jnp.full((8, BLOCK), -jnp.inf, jnp.float32)
        for first in range(0, depth, CHUNK):
            group = tiles[first : first + CHUNK]
            picked = jnp.concatenate([kv_ref[block_rows(t, BLOCK), :] for t in group], 0)
            both = lax.dot_general(
                picked, read_w[sub], (((1,), (1,)), ((), ())), preferred_element_type=jnp.float32
            )
            for j in range(len(group)):
                bias = jnp.where(first + j < live[sub], 0.0, -jnp.inf).astype(jnp.float32)
                part = both[j * BLOCK : (j + 1) * BLOCK, :BLOCK] + bias
                here = slice((first + j) * BLOCK, (first + j + 1) * BLOCK)
                scores[sub, here, :BLOCK] = part
                scores[sub, here, BLOCK:] = both[j * BLOCK : (j + 1) * BLOCK, BLOCK:]
                top = jnp.maximum(top, jnp.max(part.reshape(BLOCK // 8, 8, BLOCK), axis=0))
        return tiles, jnp.max(top, axis=0, keepdims=True)

    def weigh(sub, depth, tiles, top):
        total = jnp.zeros((8, BLOCK), jnp.float32)
        out_t = jnp.zeros((HEAD_DIM, BLOCK), jnp.float32)
        for first in range(0, depth, CHUNK):
            group = tiles[first : first + CHUNK]
            here = slice(first * BLOCK, (first + len(group)) * BLOCK)
            weight = jnp.exp2((scores[sub, here, :BLOCK] - top) * rate)
            scores[sub, here, :BLOCK] = weight
            total = total + jnp.sum(weight.reshape(-1, 8, BLOCK), axis=0)
            values_t = jnp.concatenate([kv_t[HEAD_DIM:, block_rows(t, BLOCK)] for t in group], 1)
            out_t = out_t + jnp.dot(
                values_t, weight.astype(jnp.bfloat16), preferred_element_type=jnp.float32
            )
        inverse = 1.0 / jnp.sum(total, axis=0, keepdims=True)
        out_t = (out_t * inverse).astype(jnp.bfloat16).astype(jnp.float32)
        rows = slice(sub * BLOCK, (sub + 1) * BLOCK)
        o_ref[rows, :] = out_t.T.astype(jnp.bfloat16)
        grad_t = qg_ref[rows, HEAD_DIM:].astype(jnp.float32).T
        return inverse, jnp.sum(out_t * grad_t, axis=0, keepdims=True)

    def gather_sums(sub, depth, tiles, inverse, delta):
        dq_t = jnp.zeros((HEAD_DIM, BLOCK), jnp.float32)
        for first in range(0, depth, CHUNK):
            group = tiles[first : first + CHUNK]
            here = slice(first * BLOCK, (first + len(group)) * BLOCK)
            prob = scores[sub, here, :BLOCK] * inverse
            dscore = (prob * (scores[sub, here, BLOCK:] - delta)).astype(jnp.bfloat16)
            both = jnp.concatenate([prob.astype(jnp.bfloat16), dscore], 1)
            parts = jnp.dot(both, sum_w[sub], preferred_element_type=jnp.float32)
            for j, tile in enumerate(group):
                sums[block_rows(tile, BLOCK), :] += parts[j * BLOCK : (j + 1) * BLOCK, :]
            keys_t = jnp.concatenate([kv_t[:HEAD_DIM, block_rows(t, BLOCK)] for t in group], 1)
            dq_t = dq_t + jnp.dot(keys_t, dscore, preferred_element_type=jnp.float32)
        rows = slice(sub * BLOCK, (sub + 1) * BLOCK)
        dq_ref[rows, :] = (dq_t * scaling).T.astype(jnp.bfloat16)

    def whole_pass(depth):
        found = [read(sub, depth) for sub in range(PAIR)]
        scales = [weigh(sub, depth, *found[sub]) for sub in range(PAIR)]
        for sub in range(PAIR):
            gather_sums(sub, depth, found[sub][0], *scales[sub])

    depths = sorted({slots - 2 * k for k in range(DEPTHS) if slots - 2 * k > 0})
    for k, depth in enumerate(depths):
        above = depths[k - 1] if k else 0

        @pl.when((most > above) & (most <= depth))
        def _(depth=depth):
            whole_pass(depth)

    @pl.when(step == pl.num_programs(0) - 1)
    def _():
        core = core_ref[0]

        def store(local, carry):
            shard = lax.div(local, tiles_per_shard) * 2
            within = lax.rem(local, tiles_per_shard)
            here = block_rows(local, BLOCK)
            mine = sums[block_rows((shard + core) * tiles_per_shard + within, BLOCK), :]
            other = sums[block_rows((shard + 1 - core) * tiles_per_shard + within, BLOCK), :]
            mine_ref[here, :HEAD_DIM] = mine[:, :HEAD_DIM]
            mine_ref[here, HEAD_DIM:] = mine[:, HEAD_DIM:] * scaling
            theirs_ref[here, :HEAD_DIM] = other[:, :HEAD_DIM].astype(jnp.bfloat16)
            theirs_ref[here, HEAD_DIM:] = (other[:, HEAD_DIM:] * scaling).astype(jnp.bfloat16)
            return carry

        lax.fori_loop(0, pl.num_programs(0) * PAIR, store, 0)


def on_pairs(queries, key_rows, value_rows, grad_out, tile_lists):
    tm_size, hd_size = lax.axis_size("tm"), lax.axis_size("head")
    count = tm_size // 2 * hd_size
    rows, width = queries.shape
    tile_total, slot_count = tile_lists.shape
    tiles_here = tile_total // 2
    tiles_per_shard = tile_total // tm_size
    half = count * rows
    bf16 = jnp.bfloat16
    anywhere = pl.BlockSpec(memory_space=pl.ANY)
    whole = pl.BlockSpec(memory_space=pltpu.VMEM)
    dma = pltpu.SemaphoreType.DMA
    qg, kv = pl.pallas_call(
        functools.partial(scatter_kernel, tm_size, hd_size),
        out_shape=(
            jax.ShapeDtypeStruct((half, 2 * HEAD_DIM), bf16),
            jax.ShapeDtypeStruct((2 * half, 2 * HEAD_DIM), bf16),
        ),
        in_specs=[anywhere] * 4,
        out_specs=(anywhere, anywhere),
        scratch_shapes=[
            dma((4, count)), dma((4, count)), dma((count,)), dma((count,)), dma((4,)),
        ],
        compiler_params=pltpu.CompilerParams(collective_id=0, has_side_effects=True),
        name="scatter_heads",
    )(queries, key_rows, value_rows, grad_out)

    core = lax.rem(lax.axis_index("tm"), 2)
    own_lists = jnp.where(
        core == 0,
        tile_lists.reshape(tm_size // 2, 2, tiles_per_shard, slot_count)[:, 0],
        tile_lists.reshape(tm_size // 2, 2, tiles_per_shard, slot_count)[:, 1],
    ).reshape(tiles_here, slot_count)
    live = own_lists >= 0
    slots = slot_count
    earlier = jnp.arange(slot_count)[:, None] <= jnp.arange(slot_count)[None, :]
    rank = jnp.sum(jnp.where(live[:, :, None] & earlier[None], 1, 0), axis=1) - 1
    hit = live[:, :, None] & (rank[:, :, None] == jnp.arange(slots)[None, None, :])
    lists = jnp.sum(jnp.where(hit, own_lists[:, :, None], 0), axis=1).astype(jnp.int32)
    counts = jnp.sum(live.astype(jnp.int32), axis=1)

    tile_spec = pl.BlockSpec((PAIR * BLOCK, HEAD_DIM), lambda i, *_: (i, 0))
    fixed = lambda i, *_: (0, 0)
    o, dq, mine, theirs = pl.pallas_call(
        functools.partial(attend_kernel, tiles_per_shard, slots),
        grid_spec=pltpu.PrefetchScalarGridSpec(
            num_scalar_prefetch=3,
            grid=(tiles_here // PAIR,),
            in_specs=[
                pl.BlockSpec((PAIR * BLOCK, 2 * HEAD_DIM), lambda i, *_: (i, 0)),
                pl.BlockSpec((2 * half, 2 * HEAD_DIM), fixed, pipeline_mode=pl.Buffered(1)),
            ],
            out_specs=(
                tile_spec,
                tile_spec,
                pl.BlockSpec((half, 2 * HEAD_DIM), fixed),
                pl.BlockSpec((half, 2 * HEAD_DIM), fixed),
            ),
            scratch_shapes=[
                pltpu.VMEM((2 * HEAD_DIM, 2 * half), bf16),
                pltpu.VMEM((PAIR, slots * BLOCK, 2 * BLOCK), jnp.float32),
                pltpu.VMEM((2 * half, 2 * HEAD_DIM), jnp.float32),
                pltpu.VMEM((PAIR, 2 * BLOCK, 2 * HEAD_DIM), bf16),
                pltpu.VMEM((PAIR, 2 * BLOCK, 2 * HEAD_DIM), bf16),
            ],
        ),
        out_shape=(
            jax.ShapeDtypeStruct((half, HEAD_DIM), bf16),
            jax.ShapeDtypeStruct((half, HEAD_DIM), bf16),
            jax.ShapeDtypeStruct((half, 2 * HEAD_DIM), jnp.float32),
            jax.ShapeDtypeStruct((half, 2 * HEAD_DIM), bf16),
        ),
        compiler_params=pltpu.CompilerParams(
            dimension_semantics=("arbitrary",), vmem_limit_bytes=56 * MIB
        ),
        name="attend",
    )(lists.reshape(-1), counts, core.reshape(1), qg, kv)

    out = jax.ShapeDtypeStruct((rows, width), bf16)
    return pl.pallas_call(
        functools.partial(return_kernel, tm_size, hd_size),
        out_shape=(out, out, out, out),
        in_specs=[anywhere, anywhere, whole, anywhere],
        out_specs=(anywhere,) * 4,
        scratch_shapes=[
            pltpu.VMEM((half, 2 * HEAD_DIM), bf16),
            pltpu.VMEM((half, 2 * HEAD_DIM), bf16),
            dma((4, count)), dma((4, count)), dma((count,)), dma((count,)), dma((4,)),
        ],
        compiler_params=pltpu.CompilerParams(
            collective_id=1, has_side_effects=True, vmem_limit_bytes=60 * MIB
        ),
        name="return_tokens",
    )(o, dq, mine, theirs)


def solution(mesh):
    in_specs = (
        P(("tm", "head"), None),
        P(("tm", "head"), None),
        P(("tm", "head"), None),
        P(("tm", "head"), None),
        P(),
    )
    out_specs = (
        P(("tm", "head"), None),
        P(("tm", "head"), None),
        P(("tm", "head"), None),
        P(("tm", "head"), None),
    )
    paired = mesh.shape["tm"] // 2 * mesh.shape["head"] == HEADS
    return jax.shard_map(
        on_pairs if paired else on_device, mesh=mesh, in_specs=in_specs, out_specs=out_specs, check_vma=False
    )
```
